32 devices in a mesh: ctx: 8 (over y, x, core), head: 4 (over z).
Axes of the slice: x: 2, y: 2, z: 4, core: 2. Of those that a mesh axis runs over, the one named last changes fastest.
Arguments:
- channels: bfloat16 [6144, 4096], P(('ctx', 'head')), may hold values from -6 to 6
- input_state_factors: bfloat16 [6144, 128], P(('ctx', 'head')), may hold values from -6 to 6
- c_coeffs: bfloat16 [6144, 128], P(('ctx', 'head')), may hold values from -6 to 6
- step_size_logits: bfloat16 [6144, 64], P(('ctx', 'head'))
- a_log: float32 [64], P('head')
- skip_gain: float32 [64], P('head'), may hold values from 0.5 to 1.5
- mix_gain: float32 [64, 3], P('head'), may hold values from -0.6 to 0.6
- offsets: int32 [48, 3], P('ctx'), may hold values from 1 to 3, as said below
- cotangent: bfloat16 [6144, 4096], P('ctx', 'head'), may hold values from -6 to 6
Outputs:
- mixed: bfloat16 [6144, 4096], P('ctx', 'head')
- grad_channels: bfloat16 [6144, 4096], P(('ctx', 'head'))
- grad_b: float32 [6144, 128], P(('ctx', 'head'))
- grad_c: float32 [6144, 128], P(('ctx', 'head'))
The draws below stay inside these ranges and needn't reach their ends.
Inputs may be any that keep to these rules, and one draw needn't show every extreme that they name: Each block's 3 offsets are distinct; block b's neighbour in slot k is block b - offsets[b, k], and there is none where that index is negative.
All inputs are finite; a program needn't handle non-finite values.
Results may differ from the reference program's by a relative error of at most 0.0052.
Values may be sent and summed in bfloat16 or wider, within the bound.
A program may use at most 128 MiB of HBM per device.

```python
import math
import jax
import jax.numpy as jnp
from jax import lax

H = 64
P_SIZE = 64
N = 128
Q = 128
K = 3
PATH_ELEMENTS = 6144
SPANS = 6
REACH = 3
BLOCKS = 48
N_CTX = 8


def draw_step_size_logits(key, part):
    root_random_seed, spot_key = jax.random.split(key)
    starting_displacement = jax.random.normal(root_random_seed, (PATH_ELEMENTS, H), jnp.float32)
    nonzero_block_indices = jax.random.randint(spot_key, (2,), 0, PATH_ELEMENTS)
    element_indices = jnp.arange(PATH_ELEMENTS)
    run_extent = jnp.any(element_indices[:, None] == nonzero_block_indices[None, :], axis=1)
    return jnp.where(run_extent[:, None], jnp.float32(0.8 * PATH_ELEMENTS), starting_displacement).astype(jnp.bfloat16)


def draw_a_log(key, part):
    slow_key, middle_key, fast_key, pick_key = jax.random.split(key, 4)
    slow = jnp.log(jax.random.uniform(slow_key, (H,), jnp.float32, 0.2, 0.8) / PATH_ELEMENTS)
    middle_low = jnp.log(jnp.float32(0.8 / PATH_ELEMENTS))
    middle_high = jnp.log(jnp.float32(0.12 / Q))
    middle = jax.random.uniform(middle_key, (H,), jnp.float32, 0.0, 1.0) * (middle_high - middle_low) + middle_low
    fast = jnp.log(jax.random.uniform(fast_key, (H,), jnp.float32, 1.0 / 50.0, 1.0 / 30.0))
    fast_count = H // 4
    middle_count = H // 4
    ranks = jax.random.permutation(pick_key, H)
    return jnp.where(ranks < fast_count, fast, jnp.where(ranks < fast_count + middle_count, middle, slow))


def draw_offsets(key, part):
    score_key, flag_key = jax.random.split(key)
    scores = jax.random.randint(score_key, (BLOCKS, REACH), 0, 1 << 20) * REACH + jnp.arange(REACH)[None, :]
    far_flag = jax.random.randint(flag_key, (BLOCKS,), 0, 2)
    blocks = jnp.arange(BLOCKS)
    far_flag = jnp.where(blocks == 0, 0, jnp.where(blocks == 1, 1, far_flag))
    column = jnp.arange(REACH)[None, :]
    scores = jnp.where((far_flag[:, None] == 1) & (column == REACH - 1), -1, scores)
    scores = jnp.where((far_flag[:, None] == 0) & (column == 0), -1, scores)
    order = jnp.argsort(scores, axis=1, stable=True)
    return (order[:, :K] + 1).astype(jnp.int32)


def block_scale(own_key, extent, cuts, smallest, largest):
    factor_of = 1.0
    for dim, parts in cuts:
        heights = jax.random.uniform(jax.random.fold_in(jax.random.fold_in(own_key, 6), dim), (parts,), jnp.float32, smallest / len(cuts), largest / len(cuts))
        factor_of = factor_of * jnp.repeat(jnp.exp(heights), extent[dim] // parts).reshape((-1,) + (1,) * (len(extent) - 1 - dim))
    return factor_of


def normal_values(own_key, shape, deviation, most, cuts=(), held_as=jnp.bfloat16):
    array = jax.random.normal(own_key, shape, jnp.float32) * deviation
    if len(cuts) > 0:
        array = block_scale(own_key, shape, cuts, -0.22, 0.18) * array
    return jnp.clip(array, min=-most, max=most).astype(held_as)


def setup_inputs(seed: int = 0) -> dict:
    arg_keys = jax.random.split(jax.random.key(seed), 10)
    return {
        "channels": normal_values(arg_keys[0], (PATH_ELEMENTS, H * P_SIZE), 1.0, 6.0, ((0, 32),)),
        "input_state_factors": normal_values(arg_keys[1], (PATH_ELEMENTS, N), 1.0, 6.0, ((0, 32),)),
        "c_coeffs": normal_values(arg_keys[2], (PATH_ELEMENTS, N), 1.0, 6.0, ((0, 32),)),
        "step_size_logits": draw_step_size_logits(jax.random.fold_in(arg_keys[9], 71), 0),
        "a_log": draw_a_log(jax.random.fold_in(arg_keys[9], 71), 0),
        "skip_gain": jnp.clip(1.0 + 0.1 * jax.random.normal(arg_keys[5], (H,), jnp.float32), 0.5, 1.5),
        "mix_gain": jnp.clip(jax.random.uniform(arg_keys[6], (H, K), jnp.float32, -0.6, 0.6) * block_scale(arg_keys[6], (H, K), ((0, 4),), -0.4, 0.0), -0.6, 0.6),
        "offsets": draw_offsets(jax.random.fold_in(arg_keys[9], 71), 0),
        "cotangent": normal_values(arg_keys[8], (PATH_ELEMENTS, H * P_SIZE), 1.0, 6.0, ((0, 8), (1, 4))),
    }


PRECISE = lax.Precision.HIGHEST

def straight_cast(value):
    narrow = lax.optimization_barrier(value.astype(jnp.bfloat16))
    return value + lax.stop_gradient(narrow.astype(jnp.float32) - value)

def mix_blocks(own_rows, before, offset_rows, mixing):
    neighbour_count = before.shape[0]
    blocks_in = own_rows.shape[0]
    head_count = mixing.shape[0]
    row_width = own_rows.shape[-1]
    extended = jnp.concatenate([before, own_rows], axis=0)
    result = own_rows.astype(jnp.float32)
    for column in range(offset_rows.shape[1]):
        source = (neighbour_count + jnp.arange(blocks_in, dtype=jnp.int32) - offset_rows[:, column].astype(jnp.int32)).astype(jnp.int32)
        picked = jnp.take(extended, source, axis=0)
        weight = jnp.repeat(mixing[:, column], row_width // head_count)
        result = result + weight * picked.astype(jnp.float32)
    return result

def spread_terms(grad_rows, offset_rows, neighbour_count, mixing):
    blocks_in = grad_rows.shape[0]
    head_count = mixing.shape[0]
    row_width = grad_rows.shape[-1]
    places = jnp.arange(neighbour_count + blocks_in, dtype=jnp.int32)
    result = jnp.zeros((neighbour_count + blocks_in,) + grad_rows.shape[1:], jnp.float32)
    wide_rows = grad_rows.astype(jnp.float32)
    for column in range(offset_rows.shape[1]):
        target = (neighbour_count + jnp.arange(blocks_in, dtype=jnp.int32) - offset_rows[:, column].astype(jnp.int32)).astype(jnp.int32)
        select = (target[:, None] == places[None, :]).astype(jnp.float32)
        weight = jnp.repeat(mixing[:, column], row_width // head_count)
        result = result + jnp.einsum('be,bqf->eqf', select, weight * wide_rows, precision=PRECISE)
    return result

def span_fn(state, chan, b_part, c_part, log_part, skip_gain, in_scale):
    length = log_part.shape[0]
    cum_log = jnp.cumsum(log_part, axis=0)
    scores = jnp.dot(c_part, b_part.T, precision=PRECISE) * in_scale
    causal = jnp.arange(length)[:, None] >= jnp.arange(length)[None, :]
    head_cum = cum_log.T
    log_gap = head_cum[:, :, None] - head_cum[:, None, :]
    decays = jnp.exp(jnp.where(causal[None], log_gap, -1e+30))
    weights = straight_cast(scores[None] * decays)
    y_intra = jnp.einsum('hts,shp->thp', weights, chan, precision=PRECISE)
    end_decay = jnp.exp(cum_log[-1][None, :] - cum_log)
    b_weighted = straight_cast((b_part * in_scale)[:, None, :] * end_decay[:, :, None])
    pieces = jnp.einsum('shn,shp->hpn', b_weighted, chan, precision=PRECISE)
    c_weighted = c_part[:, None, :] * jnp.exp(cum_log)[:, :, None]
    y_state = jnp.einsum('thn,hpn->thp', c_weighted, state, precision=PRECISE)
    outputs = y_intra + y_state + skip_gain[None, :, None] * chan
    return (jnp.exp(cum_log[-1])[:, None, None] * state + pieces, outputs)

def reference(channels, input_state_factors, c_coeffs, step_size_logits, a_log, skip_gain, mix_gain, offsets, cotangent):
    in_scale = 1.0 / math.sqrt(N * PATH_ELEMENTS)
    log_decay = -jnp.exp(a_log)[None, :] * jax.nn.softplus(step_size_logits.astype(jnp.float32))
    chan_g = channels.reshape(N_CTX, SPANS, Q, H, P_SIZE)
    b_g = input_state_factors.reshape(N_CTX, SPANS, Q, N)
    c_g = c_coeffs.reshape(N_CTX, SPANS, Q, N)
    log_g = log_decay.reshape(N_CTX, SPANS, Q, H)

    def run_span(state, element):
        chan, b_part, c_part, log_part = element
        new_state, outputs = span_fn(state, chan.astype(jnp.float32), b_part.astype(jnp.float32), c_part.astype(jnp.float32), log_part, skip_gain, in_scale)
        return (new_state, outputs.astype(jnp.bfloat16).reshape(Q, H * P_SIZE))

    def run_group(state, element):
        ending, rows_out = lax.scan(run_span, state, element)
        return (ending, (rows_out, state))
    zero_state = jnp.zeros((H, P_SIZE, N), jnp.float32)
    _, (out_rows, starts) = lax.scan(run_group, zero_state, (chan_g, b_g, c_g, log_g))
    before = jnp.concatenate([jnp.zeros_like(out_rows[:1, SPANS - REACH:]), out_rows[:-1, SPANS - REACH:]], axis=0)
    offset_g = offsets.reshape(N_CTX, SPANS, K)
    mixed = lax.map(lambda element: mix_blocks(element[0], element[1], element[2], mix_gain).astype(jnp.bfloat16), (out_rows, before, offset_g))
    mixed = mixed.reshape(PATH_ELEMENTS, H * P_SIZE)
    grad_g = cotangent.reshape(N_CTX, SPANS, Q, H * P_SIZE)
    later_grad = jnp.concatenate([grad_g[1:, :REACH], jnp.zeros_like(grad_g[:1, :REACH])], axis=0)
    later_offset = jnp.concatenate([offset_g[1:, :REACH], jnp.zeros_like(offset_g[:1, :REACH])], axis=0)

    def back_mix(element):
        own_grad, own_offset, next_grad, next_offset = element
        own_sums = spread_terms(own_grad, own_offset, REACH, mix_gain)
        later_sums = spread_terms(next_grad, next_offset, REACH, mix_gain)[:REACH]
        padded = jnp.concatenate([jnp.zeros((SPANS - REACH,) + later_sums.shape[1:], jnp.float32), later_sums], axis=0)
        return (own_grad.astype(jnp.float32) + own_sums[REACH:] + padded).astype(jnp.bfloat16)
    grad_out = lax.map(back_mix, (grad_g, offset_g, later_grad, later_offset))
    grad_spans = grad_out.reshape(N_CTX, SPANS, Q, H, P_SIZE)

    def back_group(grad_end, element):
        chan_c, b_c, c_c, log_c, start_state, grad_part_g = element

        def replay(state, piece_in):
            chan, b_part, c_part, log_part = piece_in
            new_state, _ = span_fn(state, chan.astype(jnp.float32), b_part.astype(jnp.float32), c_part.astype(jnp.float32), log_part, skip_gain, in_scale)
            return (new_state, state)
        _, states = lax.scan(replay, start_state, (chan_c, b_c, c_c, log_c))

        def backward_offset(grad_after, piece_in):
            chan, b_part, c_part, log_part, state, grad_part = piece_in

            def span_local(chan_f, b_f, c_f, state_f):
                return span_fn(state_f, chan_f, b_f, c_f, log_part, skip_gain, in_scale)
            _, pull = jax.vjp(span_local, chan.astype(jnp.float32), b_part.astype(jnp.float32), c_part.astype(jnp.float32), state)
            feature_derivative, b_grad, c_grad, state_grad = pull((grad_after, grad_part.astype(jnp.float32)))
            return (state_grad, (feature_derivative.astype(jnp.bfloat16).reshape(Q, H * P_SIZE), b_grad, c_grad))
        grad_start, results = lax.scan(backward_offset, grad_end, (chan_c, b_c, c_c, log_c, states, grad_part_g), reverse=True)
        return (grad_start, results)
    _, (grad_x, grad_b, grad_c) = lax.scan(back_group, zero_state, (chan_g, b_g, c_g, log_g, starts, grad_spans), reverse=True)
    return (mixed, grad_x.reshape(PATH_ELEMENTS, H * P_SIZE), grad_b.reshape(PATH_ELEMENTS, N), grad_c.reshape(PATH_ELEMENTS, N))
```

```python
import math

import jax
import jax.numpy as jnp
from jax import lax
from jax.experimental import pallas as pl
from jax.experimental.pallas import tpu as pltpu
from jax.sharding import PartitionSpec as P

P_SIZE = 64
N = 128
Q = 128
F32 = jnp.float32
BF16 = jnp.bfloat16
VMEM_BYTES = 48 * 1024 * 1024


def dot(left, right, dims, precision=None):
    return lax.dot_general(
        left, right, (dims, ((), ())), preferred_element_type=F32, precision=precision
    )


def iota(shape, dim):
    return lax.broadcasted_iota(jnp.int32, shape, dim)


def halves(value):
    high = value.astype(BF16)
    return high, (value - high.astype(F32)).astype(BF16)


def head_of_column(heads):
    return (iota((heads, heads * P_SIZE), 1) // P_SIZE == iota((heads, heads * P_SIZE), 0)).astype(
        F32
    ).astype(BF16)


def over_columns(value, spread):
    high, low = halves(value)
    return dot(high, spread, ((1,), (0,))) + dot(low, spread, ((1,), (0,)))


def over_rows(column, spread):
    high, low = halves(jnp.broadcast_to(column, (column.shape[0], N)))
    return dot(spread, high, ((0,), (0,))) + dot(spread, low, ((0,), (0,)))


def two_heads(value):
    lower = iota(value.shape, 1) < P_SIZE
    zero = jnp.zeros_like(value)
    return jnp.concatenate([jnp.where(lower, value, zero), jnp.where(lower, zero, value)], axis=0)


def call(kernel, outs, args, grid=None, in_specs=None, out_specs=None, scratch=(), cost=0):
    moved = sum(a.size * a.dtype.itemsize for a in args) + sum(
        math.prod(o.shape) * o.dtype.itemsize for o in outs
    )
    extra = {} if grid is None else {"grid": grid}
    whole = pl.BlockSpec(memory_space=pltpu.VMEM)
    return pl.pallas_call(
        kernel,
        out_shape=outs,
        in_specs=in_specs or [whole] * len(args),
        out_specs=out_specs or [whole] * len(outs),
        scratch_shapes=scratch,
        compiler_params=pltpu.CompilerParams(vmem_limit_bytes=VMEM_BYTES),
        cost_estimate=pl.CostEstimate(flops=cost, bytes_accessed=moved, transcendentals=0),
        **extra,
    )(*args)


def shaped(shape, dtype):
    return jax.ShapeDtypeStruct(shape, dtype)


def back_mix_kernel(
    spans, reach, dt, a_log, coeffs, cot, later, gains, g_out, cum_out, cumt_out, full_out, end_out
):
    heads = dt.shape[1]
    pad = end_out.shape[0] - heads * P_SIZE
    spread = head_of_column(heads)
    tri = (iota((Q, Q), 0) >= iota((Q, Q), 1)).astype(F32)
    rate = -jnp.exp(a_log[...])
    earlier = jnp.zeros((heads, 1), F32)
    grad_in = jnp.zeros((heads * P_SIZE, N), F32)
    for span in range(spans):
        rows = pl.ds(span * Q, Q)
        decay = rate * jax.nn.softplus(dt[rows, :].astype(F32))
        cum = dot(tri, decay, ((1,), (0,)), lax.Precision.HIGHEST)
        cumt = dot(decay, tri, ((0,), (1,)), lax.Precision.HIGHEST)
        cum_out[rows, :] = cum
        cumt_out[span] = cumt
        grad = cot[rows, :].astype(F32)
        for far in range(reach):
            place = span + far + 1
            if place < spans:
                block = cot[pl.ds(place * Q, Q), :]
            else:
                block = later[pl.ds((place - spans) * Q, Q), :]
            grad = grad + gains[span, far : far + 1, :] * block.astype(F32)
        grad = grad.astype(BF16)
        g_out[rows, :] = grad
        scaled = (grad.astype(F32) * over_columns(jnp.exp(cum), spread)).astype(BF16)
        full = dot(scaled, coeffs[rows, N : 2 * N], ((0,), (0,)))
        full_out[span] = full.astype(BF16)
        grad_in = grad_in + over_rows(jnp.exp(earlier), spread) * full
        earlier = earlier + cumt[:, Q - 1 : Q]
    end_out[: heads * P_SIZE, :] = grad_in.astype(BF16)
    total = jnp.broadcast_to(earlier, (heads, N))
    high, low = halves(total)
    lowest = (total - high.astype(F32) - low.astype(F32)).astype(BF16)
    lane = iota((heads, N), 1)
    packed = jnp.where(lane == 0, high, jnp.where(lane == 1, low, lowest))
    if pad > heads:
        packed = jnp.concatenate([packed, jnp.zeros((pad - heads, N), BF16)], axis=0)
    end_out[heads * P_SIZE :, :] = packed


def carried(place, logs, values, reverse, heads, spread):
    count = logs.shape[0]
    running = jnp.zeros((heads, 1), F32)
    result = jnp.zeros((heads * P_SIZE, N), F32)
    for step in range(count):
        source = step if reverse else count - 1 - step
        ahead = (source > place) if reverse else (source < place)
        use = jnp.where(ahead, 1.0, 0.0).astype(F32)
        result = result + over_rows(use * jnp.exp(running), spread) * values[
            source, : heads * P_SIZE, :
        ].astype(F32)
        packed = logs[source, :heads, :].astype(F32)
        running = running + use * (packed[:, 0:1] + packed[:, 1:2] + packed[:, 2:3])
    return result


def grad_channels_kernel(
    in_scale, place, ends, cum, cumt, coeffs, g, full, skip, dx_out, pieces_out, carry
):
    heads = cum.shape[1]
    spread = head_of_column(heads)

    @pl.when(pl.program_id(0) == 0)
    def _():
        carry[...] = carried(
            place[0], ends.at[:, pl.ds(heads * P_SIZE, ends.shape[1] - heads * P_SIZE), :], ends, True, heads, spread
        )

    after = carry[...]
    pieces = after.astype(BF16)
    pieces_out[0] = pieces
    b_rows = coeffs[:, :N]
    c_rows = coeffs[:, N : 2 * N]
    end = jnp.exp(cumt[0][:, Q - 1 : Q])
    tail = jnp.exp(cum[Q - 1 : Q, :] - cum[...]) * in_scale
    from_state = dot(b_rows, pieces, ((1,), (1,))) * over_columns(tail, spread)
    scores = dot(b_rows, c_rows, ((1,), (1,))) * in_scale
    seen = iota((Q, Q), 0) <= iota((Q, Q), 1)
    for pair in range(heads // 2):
        columns = slice(pair * 2 * P_SIZE, (pair + 1) * 2 * P_SIZE)
        weights = []
        for head in (2 * pair, 2 * pair + 1):
            gap = cumt[0][head : head + 1, :] - cum[:, head : head + 1]
            weights.append((scores * jnp.exp(jnp.where(seen, gap, -1e30))).astype(BF16))
        grads = g[:, columns]
        intra = dot(jnp.concatenate(weights, axis=1), two_heads(grads), ((1,), (0,)))
        dx_out[:, columns] = (
            intra + from_state[:, columns] + skip[:, columns] * grads.astype(F32)
        ).astype(BF16)
    carry[...] = full[0].astype(F32) + over_rows(end, spread) * after


def pieces_kernel(in_scale, cum, cumt, coeffs, chan, starts_out, end_out, carry):
    heads = cum.shape[1]
    spread = head_of_column(heads)

    @pl.when(pl.program_id(0) == 0)
    def _():
        carry[...] = jnp.zeros_like(carry)

    state = carry[...]
    starts_out[0] = state
    tail = jnp.exp(cum[Q - 1 : Q, :] - cum[...]) * in_scale
    scaled = (chan[...].astype(F32) * over_columns(tail, spread)).astype(BF16)
    pieces = dot(scaled, coeffs[:, :N], ((0,), (0,)))
    state = over_rows(jnp.exp(cumt[0][:, Q - 1 : Q]), spread) * state + pieces
    carry[...] = state
    end_out[...] = state.astype(BF16)


def intra_kernel(in_scale, cum, cumt, coeffs, chan, g, pieces, skip, y_out, db_out, dc_out):
    heads = cum.shape[1]
    spread = head_of_column(heads)
    b_rows = coeffs[:, :N]
    c_rows = coeffs[:, N : 2 * N]
    scores = dot(c_rows, b_rows, ((1,), (1,))) * in_scale
    seen = iota((Q, Q), 0) >= iota((Q, Q), 1)
    score_grads = jnp.zeros((Q, Q), F32)
    for pair in range(heads // 2):
        columns = slice(pair * 2 * P_SIZE, (pair + 1) * 2 * P_SIZE)
        chans = chan[:, columns]
        products = dot(two_heads(g[:, columns]), chans, ((1,), (1,)))
        weights = []
        for one, head in enumerate((2 * pair, 2 * pair + 1)):
            gap = cum[:, head : head + 1] - cumt[0][head : head + 1, :]
            decay = jnp.exp(jnp.where(seen, gap, -1e30))
            weights.append((scores * decay).astype(BF16))
            score_grads = score_grads + products[one * Q : (one + 1) * Q, :] * decay
        y_out[:, columns] = (
            dot(jnp.concatenate(weights, axis=1), two_heads(chans), ((1,), (0,)))
            + skip[:, columns] * chans.astype(F32)
        )
    score_grads = (score_grads * in_scale).astype(BF16)
    tail = jnp.exp(cum[Q - 1 : Q, :] - cum[...]) * in_scale
    scaled = (chan[...].astype(F32) * over_columns(tail, spread)).astype(BF16)
    dc_out[...] = dot(score_grads, b_rows, ((1,), (0,)))
    db_out[...] = dot(score_grads, c_rows, ((0,), (0,))) + dot(scaled, pieces[0], ((1,), (0,)))


def outputs_kernel(
    place, logs, ends, cum, cumt, coeffs, g, starts, y_intra, db, dc, out, grads_out, entering, passed
):
    heads = cum.shape[1]
    spread = head_of_column(heads)

    @pl.when(pl.program_id(0) == 0)
    def _():
        entering[...] = carried(place[0], logs, ends, False, heads, spread)

    state = entering[...]
    full = (starts[0] + state).astype(BF16)
    grown = over_columns(jnp.exp(cum[...]), spread)
    out[...] = (
        y_intra[...] + dot(coeffs[:, N : 2 * N], full, ((1,), (1,))) * grown
    ).astype(BF16)
    scaled = (g[...].astype(F32) * grown).astype(BF16)
    grads_out[:, :N] = db[...].astype(BF16)
    grads_out[:, N:] = (dc[...] + dot(scaled, full, ((1,), (0,)))).astype(BF16)
    entering[...] = over_rows(jnp.exp(cumt[0][:, Q - 1 : Q]), spread) * state


def mix_kernel(spans, reach, own, before, gains, mixed):
    for span in range(spans):
        rows = pl.ds(span * Q, Q)
        result = own[rows, :].astype(F32)
        for far in range(reach):
            place = span - far - 1
            if place >= 0:
                block = own[pl.ds(place * Q, Q), :]
            else:
                block = before[pl.ds((place + reach) * Q, Q), :]
            result = result + gains[span, far : far + 1, :] * block.astype(F32)
        mixed[rows, :] = result.astype(BF16)


def passed_along(value, axis, steps):
    count = lax.axis_size(axis)
    first, last = (max(0, -steps), min(count, count - steps))
    return lax.ppermute(value, axis, [(source, source + steps) for source in range(first, last)])


def exchanged(pieces, axis):
    count = lax.axis_size(axis)
    me = lax.axis_index(axis)
    arrived = [lax.dynamic_index_in_dim(pieces, me, 0, True)]
    for shift in range(1, count):
        sent = lax.dynamic_index_in_dim(pieces, (me + shift) % count, 0, True)
        pairs = [(source, (source + shift) % count) for source in range(count)]
        arrived.append(lax.ppermute(sent, axis, pairs))
    result = jnp.zeros_like(pieces)
    for shift in range(count):
        result = lax.dynamic_update_slice_in_dim(
            result, arrived[shift], (me + count - shift) % count, 0
        )
    return result


def body(channels, b_own, c_own, dt_own, a_log, skip_gain, mix_gain, offsets, cotangent):
    groups = lax.axis_size("head")
    ctx = lax.axis_size("ctx")
    tok_dev = channels.shape[0]
    ctx_tok = tok_dev * groups
    spans = ctx_tok // Q
    reach = spans // 2
    heads = a_log.shape[0]
    width = heads * P_SIZE
    in_scale = 1.0 / math.sqrt(N * ctx_tok * ctx)
    place = lax.axis_index("ctx").astype(jnp.int32).reshape(1)

    small = jnp.concatenate([b_own, c_own, dt_own], axis=1)
    gathered = lax.all_gather(small, "head", axis=0, tiled=True)
    later = passed_along(cotangent[: reach * Q], "ctx", -1)
    later_offsets = passed_along(offsets[:reach], "ctx", -1)
    sent = channels.reshape(tok_dev, groups, width).transpose(1, 0, 2)
    gathered, sent = lax.optimization_barrier((gathered, sent))
    chan = exchanged(sent, "head").reshape(ctx_tok, width)

    coeffs = gathered[:, : 2 * N]
    dt = lax.dynamic_slice_in_dim(gathered, 2 * N + lax.axis_index("head") * heads, heads, axis=1)
    skip = jnp.repeat(skip_gain, P_SIZE)[None, :]
    distance = jnp.arange(1, reach + 1, dtype=jnp.int32)
    near = (offsets[:, None, :] == distance[None, :, None]).astype(F32)
    wide_gain = jnp.repeat(mix_gain, P_SIZE, axis=0)
    forward_gains = jnp.sum(near[:, :, None, :] * wide_gain[None, None], axis=-1)
    all_offsets = jnp.concatenate([offsets, later_offsets], axis=0)
    at = jnp.stack([all_offsets[far : far + spans] for far in range(1, reach + 1)], axis=1)
    back = (at == distance[None, :, None]).astype(F32)
    back_gains = jnp.sum(back[:, :, None, :] * wide_gain[None, None], axis=-1)

    pad = -(-heads // 16) * 16
    unit = 2 * ctx_tok * width * N
    g, cum, cumt, full, end_grad = call(
        lambda *refs: back_mix_kernel(spans, reach, *refs),
        [
            shaped((ctx_tok, width), BF16),
            shaped((ctx_tok, heads), F32),
            shaped((spans, heads, Q), F32),
            shaped((spans, width, N), BF16),
            shaped((width + pad, N), BF16),
        ],
        (dt, a_log[None, :], coeffs, cotangent, later, back_gains),
        cost=60 * unit,
    )
    grad_ends = lax.all_gather(end_grad, "ctx")

    def rows_at(order):
        def rows(columns):
            return pl.BlockSpec((Q, columns), lambda i: (order(i), 0))

        def planes(extent):
            return pl.BlockSpec((1,) + extent, lambda i: (order(i), 0, 0))

        return rows, planes

    fixed = pl.BlockSpec(memory_space=pltpu.VMEM)
    scalar = pl.BlockSpec(memory_space=pltpu.SMEM)
    rows, planes = rows_at(lambda i: spans - 1 - i)
    dx, pieces = call(
        lambda *refs: grad_channels_kernel(in_scale, *refs),
        [shaped((ctx_tok, width), BF16), shaped((spans, width, N), BF16)],
        (place, grad_ends, cum, cumt, coeffs, g, full, skip),
        grid=(spans,),
        in_specs=[
            scalar, fixed, rows(heads), planes((heads, Q)), rows(2 * N), rows(width),
            planes((width, N)), fixed,
        ],
        out_specs=[rows(width), planes((width, N))],
        scratch=[pltpu.VMEM((width, N), F32)],
        cost=60 * unit,
    )
    chan, dx = lax.optimization_barrier((chan, dx))
    dx = exchanged(dx.reshape(groups, tok_dev, width), "head")
    grad_channels = dx.transpose(1, 0, 2).reshape(tok_dev, groups * width)

    rows, planes = rows_at(lambda i: i)
    starts, end_state = call(
        lambda *refs: pieces_kernel(in_scale, *refs),
        [shaped((spans, width, N), F32), shaped((width, N), BF16)],
        (cum, cumt, coeffs, chan),
        grid=(spans,),
        in_specs=[rows(heads), planes((heads, Q)), rows(2 * N), rows(width)],
        out_specs=[planes((width, N)), pl.BlockSpec((width, N), lambda i: (0, 0))],
        scratch=[pltpu.VMEM((width, N), F32)],
        cost=30 * unit,
    )
    end_states = lax.all_gather(end_state, "ctx")
    y_intra, db, dc = call(
        lambda *refs: intra_kernel(in_scale, *refs),
        [shaped((ctx_tok, width), F32), shaped((ctx_tok, N), F32), shaped((ctx_tok, N), F32)],
        (cum, cumt, coeffs, chan, g, pieces, skip),
        grid=(spans,),
        in_specs=[
            rows(heads), planes((heads, Q)), rows(2 * N), rows(width), rows(width),
            planes((width, N)), fixed,
        ],
        out_specs=[rows(width), rows(N), rows(N)],
        cost=60 * unit,
    )
    logs = grad_ends[:, width:, :]
    out, coeff_grads = call(
        outputs_kernel,
        [shaped((ctx_tok, width), BF16), shaped((ctx_tok, 2 * N), BF16)],
        (place, logs, end_states, cum, cumt, coeffs, g, starts, y_intra, db, dc),
        grid=(spans,),
        in_specs=[
            scalar, fixed, fixed, rows(heads), planes((heads, Q)), rows(2 * N), rows(width),
            planes((width, N)), rows(width), rows(N), rows(N),
        ],
        out_specs=[rows(width), rows(2 * N)],
        scratch=[pltpu.VMEM((width, N), F32), pltpu.VMEM((8, N), F32)],
        cost=60 * unit,
    )
    before = passed_along(out[(spans - reach) * Q :], "ctx", 1)
    parts = lax.all_to_all(
        coeff_grads.reshape(groups, tok_dev, 2 * N), "head", split_axis=0, concat_axis=0
    )
    (mixed,) = call(
        lambda *refs: mix_kernel(spans, reach, *refs),
        [shaped((ctx_tok, width), BF16)],
        (out, before, forward_gains),
        cost=30 * unit,
    )
    summed = jnp.sum(parts.astype(F32), axis=0)
    return (mixed, grad_channels, summed[:, :N], summed[:, N:])


def solution(mesh):
    by_token = P(("ctx", "head"), None)
    return jax.shard_map(
        body,
        mesh=mesh,
        in_specs=(
            by_token, by_token, by_token, by_token, P("head"), P("head"), P("head", None),
            P("ctx", None), P("ctx", "head"),
        ),
        out_specs=(P("ctx", "head"), by_token, by_token, by_token),
        check_vma=False,
    )
```

```python
import math

import jax
import jax.numpy as jnp
from jax import lax
from jax.experimental import pallas as pl
from jax.experimental.pallas import tpu as pltpu
from jax.sharding import PartitionSpec as P

P_SIZE = 64
N = 128
Q = 128
F32 = jnp.float32
BF16 = jnp.bfloat16
VMEM_BYTES = 56 * 1024 * 1024


def dot(left, right, dims, precision=None):
    return lax.dot_general(
        left, right, (dims, ((), ())), preferred_element_type=F32, precision=precision
    )


def iota(shape, dim):
    return lax.broadcasted_iota(jnp.int32, shape, dim)


def halves(value):
    high = value.astype(BF16)
    return high, (value - high.astype(F32)).astype(BF16)


def head_of_column(heads):
    shape = (heads, heads * P_SIZE)
    first = iota(shape, 0) * P_SIZE
    column = iota(shape, 1)
    return ((column >= first) & (column < first + P_SIZE)).astype(F32).astype(BF16)


def over_columns(value, spread):
    high, low = halves(value)
    return dot(high, spread, ((1,), (0,))) + dot(low, spread, ((1,), (0,)))


def over_rows(column, spread):
    high, low = halves(jnp.broadcast_to(column, (column.shape[0], N)))
    return dot(spread, high, ((0,), (0,))) + dot(spread, low, ((0,), (0,)))


def two_heads(value):
    lower = iota(value.shape, 1) < P_SIZE
    zero = jnp.zeros_like(value)
    return jnp.concatenate([jnp.where(lower, value, zero), jnp.where(lower, zero, value)], axis=0)


def remote(source, target, send, recv, axis, place):
    return pltpu.make_async_remote_copy(
        src_ref=source,
        dst_ref=target,
        send_sem=send,
        recv_sem=recv,
        device_id={axis: place},
        device_id_type=pl.DeviceIdType.MESH,
    )


def mixer_kernel(
    groups, ctx, spans, reach, in_scale,
    chan_in, b_in, c_in, dt_in, a_log, skip, gain, offs, cot_in,
    mixed, gx, gb, gc,
    cot, off, b_all, c_all, dt_all, chan, g, cum_all, cumt_all, full, pay_g, ends_g, pay_s, ends_s,
    pieces, dx, starts, y_intra, db, dc, grads, parts, out, carry, running,
    z_send, z_recv, c_send, c_recv, n_send, n_recv, local,
):
    heads = a_log.shape[1]
    width = heads * P_SIZE
    tok_dev = chan_in.shape[0]
    slots = gain.shape[0]
    me = lax.axis_index("head")
    place = lax.axis_index("ctx")
    spread = head_of_column(heads)

    def token_rows(index):
        return pl.ds(pl.multiple_of(index * tok_dev, 64), tok_dev)

    def wide(index):
        return pl.ds(pl.multiple_of(index * width, 128), width)

    def span_rows(span):
        return pl.ds(pl.multiple_of(span * Q, Q), Q)

    barrier = pltpu.get_barrier_semaphore()
    for shift in range(1, groups):
        pl.semaphore_signal(
            barrier, inc=1, device_id={"head": lax.rem(me + shift, groups)},
            device_id_type=pl.DeviceIdType.MESH,
        )
    for shift in range(1, ctx):
        pl.semaphore_signal(
            barrier, inc=1, device_id={"ctx": lax.rem(place + shift, ctx)},
            device_id_type=pl.DeviceIdType.MESH,
        )
    own = [
        pltpu.make_async_copy(b_in, b_all.at[token_rows(me), :], local.at[0]),
        pltpu.make_async_copy(c_in, c_all.at[token_rows(me), :], local.at[1]),
        pltpu.make_async_copy(dt_in, dt_all.at[token_rows(me), :], local.at[2]),
        pltpu.make_async_copy(cot_in, cot.at[pl.ds(0, spans * Q), :], local.at[3]),
        pltpu.make_async_copy(offs, off.at[pl.ds(0, spans)], local.at[4]),
        pltpu.make_async_copy(chan_in.at[:, wide(me)], chan.at[token_rows(me), :], local.at[5]),
    ]
    for copy in own:
        copy.start()
    pl.semaphore_wait(barrier, groups - 1 + ctx - 1)

    small, large = [], []
    for shift in range(1, groups):
        target = lax.rem(me + shift, groups)
        for kind, (source, home) in enumerate(((b_in, b_all), (c_in, c_all), (dt_in, dt_all))):
            small.append(
                remote(
                    source, home.at[token_rows(me), :], z_send.at[kind, shift],
                    z_recv.at[kind, shift], "head", target,
                )
            )
        large.append(
            remote(
                chan_in.at[:, wide(target)], chan.at[token_rows(me), :], z_send.at[3, shift],
                z_recv.at[3, shift], "head", target,
            )
        )
    back = lax.rem(place + ctx - 1, ctx)
    onward = lax.rem(place + 1, ctx)
    later = [
        remote(
            offs.at[pl.ds(0, reach)], off.at[pl.ds(spans, reach)], n_send.at[0], n_recv.at[0],
            "ctx", back,
        ),
        remote(
            cot_in.at[pl.ds(0, reach * Q), :], cot.at[pl.ds(spans * Q, reach * Q), :],
            n_send.at[1], n_recv.at[1], "ctx", back,
        ),
    ]
    for copy in small:
        copy.start()

    @pl.when(place > 0)
    def _():
        for copy in later:
            copy.start()

    for copy in large:
        copy.start()

    @pl.when(place == 0)
    def _():
        out[pl.ds(0, reach * Q), :] = jnp.zeros((reach * Q, width), BF16)

    @pl.when(place == ctx - 1)
    def _():
        cot[pl.ds(spans * Q, reach * Q), :] = jnp.zeros((reach * Q, width), BF16)
        off[pl.ds(spans, reach)] = jnp.zeros((reach, 1, N), jnp.int32)

    for copy in own[:5]:
        copy.wait()
    for copy in small:
        copy.wait_recv()

    chosen = (
        iota((dt_all.shape[1], heads), 0) == iota((dt_all.shape[1], heads), 1) + me * heads
    ).astype(F32).astype(BF16)
    tri = (iota((Q, Q), 0) >= iota((Q, Q), 1)).astype(F32)
    rate = -jnp.exp(a_log[...])

    def add_up(span, total):
        rows = span_rows(span)
        steps = dot(dt_all[rows, :], chosen, ((1,), (0,)))
        decay = rate * (jnp.maximum(steps, 0.0) + jnp.log1p(jnp.exp(-jnp.abs(steps))))
        cumt = dot(decay, tri, ((0,), (1,)), lax.Precision.HIGHEST)
        cum_all[rows, :] = dot(tri, decay, ((1,), (0,)), lax.Precision.HIGHEST)
        cumt_all[span] = cumt
        return total + cumt[:, Q - 1 : Q]

    total = lax.fori_loop(0, spans, add_up, jnp.zeros((heads, 1), F32))
    high, low = halves(jnp.broadcast_to(total, (heads, N)))
    lowest = (total - high.astype(F32) - low.astype(F32)).astype(BF16)
    lane = iota((heads, N), 1)
    packed = jnp.where(lane == 0, high, jnp.where(lane == 1, low, lowest))
    pad = pay_g.shape[0] - width
    if pad > heads:
        packed = jnp.concatenate([packed, jnp.zeros((pad - heads, N), BF16)], axis=0)
    pay_g[pl.ds(width, pad), :] = packed
    pay_s[pl.ds(width, pad), :] = packed

    @pl.when(place < ctx - 1)
    def _():
        for copy in later:
            copy.wait_recv()

    def picked(row, far):
        offset = off[row]
        weight = jnp.zeros((1, width), F32)
        for slot in range(slots):
            hit = (offset[:, slot : slot + 1] == far).astype(F32)
            weight = weight + hit * gain[slot : slot + 1, :]
        return weight

    carry[...] = jnp.zeros_like(carry)

    def back_mix(span, earlier):
        rows = span_rows(span)
        grad = cot[rows, :].astype(F32)
        for far in range(1, reach + 1):
            grad = grad + picked(span + far, far) * cot[span_rows(span + far), :].astype(F32)
        grad = grad.astype(BF16)
        g[rows, :] = grad
        scaled = (grad.astype(F32) * over_columns(jnp.exp(cum_all[rows, :]), spread)).astype(BF16)
        flow = dot(scaled, c_all[rows, :], ((0,), (0,)))
        full[span] = flow.astype(BF16)
        carry[...] = carry[...] + over_rows(jnp.exp(earlier), spread) * flow
        return earlier + cumt_all[span][:, Q - 1 : Q]

    lax.fori_loop(0, spans, back_mix, jnp.zeros((heads, 1), F32))
    pay_g[pl.ds(0, width), :] = carry[...].astype(BF16)

    def scan_copies(kind, source, ends, sign):
        return [
            remote(
                source, ends.at[far - 1], c_send.at[kind, far], c_recv.at[kind, far], "ctx",
                lax.rem(place + ctx + sign * far, ctx),
            )
            for far in range(1, ctx)
        ]

    to_earlier = scan_copies(0, pay_g, ends_g, -1)
    to_later = scan_copies(1, pay_s, ends_s, 1)

    def gather_ends(ends, copies, present):
        carry[...] = jnp.zeros_like(carry)
        running[...] = jnp.zeros_like(running)
        for far in range(1, ctx):

            @pl.when(present(far))
            def _(far=far):
                copies[far - 1].wait_recv()
                sums = running[...]
                carry[...] = carry[...] + over_rows(jnp.exp(sums[:, :1]), spread) * ends[
                    far - 1, pl.ds(0, width), :
                ].astype(F32)
                logs = ends[far - 1, pl.ds(width, pad), :].astype(F32)[:heads]
                running[...] = sums + (logs[:, 0:1] + logs[:, 1:2] + logs[:, 2:3])

    for far in range(1, ctx):

        @pl.when(place >= far)
        def _(far=far):
            to_earlier[far - 1].start()

    own[5].wait()
    for copy in large:
        copy.wait_recv()

    def tail_of(rows):
        cum = cum_all[rows, :]
        last = cum[Q - 1 : Q, :]
        return over_columns(jnp.exp(last - cum) * in_scale, spread)

    carry[...] = jnp.zeros_like(carry)

    def add_pieces(span, unused):
        rows = span_rows(span)
        state = carry[...]
        starts[span] = state
        scaled = (chan[rows, :].astype(F32) * tail_of(rows)).astype(BF16)
        added = dot(scaled, b_all[rows, :], ((0,), (0,)))
        carry[...] = over_rows(jnp.exp(cumt_all[span][:, Q - 1 : Q]), spread) * state + added
        return unused

    lax.fori_loop(0, spans, add_pieces, 0)
    pay_s[pl.ds(0, width), :] = carry[...].astype(BF16)
    for far in range(1, ctx):

        @pl.when(place + far < ctx)
        def _(far=far):
            to_later[far - 1].start()

    gather_ends(ends_g, to_earlier, lambda far: place + far < ctx)

    def dx_copy(chunk):
        return remote(
            dx.at[pl.ds(chunk * tok_dev, tok_dev), :], gx.at[:, wide(me)], z_send.at[4, chunk],
            z_recv.at[4, me], "head", chunk,
        )

    def grad_channels(step, unused):
        span = spans - 1 - step
        rows = span_rows(span)
        after = carry[...]
        flow = after.astype(BF16)
        pieces[span] = flow
        b_rows = b_all[rows, :]
        cum = cum_all[rows, :]
        cumt = cumt_all[span]
        from_state = dot(b_rows, flow, ((1,), (1,))) * tail_of(rows)
        scores = dot(b_rows, c_all[rows, :], ((1,), (1,))) * in_scale
        seen = iota((Q, Q), 0) <= iota((Q, Q), 1)
        for pair in range(heads // 2):
            columns = slice(pair * 2 * P_SIZE, (pair + 1) * 2 * P_SIZE)
            weights = []
            for head in (2 * pair, 2 * pair + 1):
                gap = cumt[head : head + 1, :] - cum[:, head : head + 1]
                weights.append((scores * jnp.exp(jnp.where(seen, gap, -1e30))).astype(BF16))
            part = g[rows, columns]
            intra = dot(jnp.concatenate(weights, axis=1), two_heads(part), ((1,), (0,)))
            dx[rows, columns] = (
                intra + from_state[:, columns] + skip[:, columns] * part.astype(F32)
            ).astype(BF16)
        carry[...] = full[span].astype(F32) + over_rows(jnp.exp(cumt[:, Q - 1 : Q]), spread) * after
        for chunk in range(groups):

            @pl.when((span == chunk * tok_dev // Q) & (me != chunk))
            def _(chunk=chunk):
                dx_copy(chunk).start()

        return unused

    lax.fori_loop(0, spans, grad_channels, 0)
    keep = pltpu.make_async_copy(dx.at[token_rows(me), :], gx.at[:, wide(me)], local.at[6])
    keep.start()

    def intra(span, unused):
        rows = span_rows(span)
        b_rows = b_all[rows, :]
        c_rows = c_all[rows, :]
        cum = cum_all[rows, :]
        cumt = cumt_all[span]
        scores = dot(c_rows, b_rows, ((1,), (1,))) * in_scale
        seen = iota((Q, Q), 0) >= iota((Q, Q), 1)
        score_grads = jnp.zeros((Q, Q), F32)
        for pair in range(heads // 2):
            columns = slice(pair * 2 * P_SIZE, (pair + 1) * 2 * P_SIZE)
            chans = chan[rows, columns]
            products = dot(two_heads(g[rows, columns]), chans, ((1,), (1,)))
            weights = []
            for one, head in enumerate((2 * pair, 2 * pair + 1)):
                gap = cum[:, head : head + 1] - cumt[head : head + 1, :]
                decay = jnp.exp(jnp.where(seen, gap, -1e30))
                weights.append((scores * decay).astype(BF16))
                score_grads = score_grads + products[one * Q : (one + 1) * Q, :] * decay
            y_intra[rows, columns] = dot(
                jnp.concatenate(weights, axis=1), two_heads(chans), ((1,), (0,))
            ) + skip[:, columns] * chans.astype(F32)
        score_grads = (score_grads * in_scale).astype(BF16)
        scaled = (chan[rows, :].astype(F32) * tail_of(rows)).astype(BF16)
        dc[rows, :] = dot(score_grads, b_rows, ((1,), (0,)))
        db[rows, :] = dot(score_grads, c_rows, ((0,), (0,))) + dot(
            scaled, pieces[span], ((1,), (0,))
        )
        return unused

    lax.fori_loop(0, spans, intra, 0)

    gather_ends(ends_s, to_later, lambda far: place >= far)

    def before_copy(block):
        return remote(
            out.at[pl.ds((spans + block) * Q, Q), :], out.at[pl.ds(block * Q, Q), :],
            n_send.at[2 + block], n_recv.at[2 + block], "ctx", onward,
        )

    def outputs(span, unused):
        rows = span_rows(span)
        state = carry[...]
        whole = (starts[span] + state).astype(BF16)
        grown = over_columns(jnp.exp(cum_all[rows, :]), spread)
        out[span_rows(span + reach), :] = (
            y_intra[rows, :] + dot(c_all[rows, :], whole, ((1,), (1,))) * grown
        ).astype(BF16)
        for block in range(reach):

            @pl.when((span == spans - reach + block) & (place < ctx - 1))
            def _(block=block):
                before_copy(block).start()

        scaled = (g[rows, :].astype(F32) * grown).astype(BF16)
        grads[rows, pl.ds(0, N)] = db[rows, :].astype(BF16)
        grads[rows, pl.ds(N, N)] = (dc[rows, :] + dot(scaled, whole, ((1,), (0,)))).astype(BF16)
        carry[...] = over_rows(jnp.exp(cumt_all[span][:, Q - 1 : Q]), spread) * state
        return unused

    lax.fori_loop(0, spans, outputs, 0)
    shares = [
        remote(
            grads.at[token_rows(lax.rem(me + shift, groups)), :], parts.at[shift - 1],
            z_send.at[5, shift], z_recv.at[5, shift], "head", lax.rem(me + shift, groups),
        )
        for shift in range(1, groups)
    ]
    for copy in shares:
        copy.start()

    def mix(span, unused):
        own_rows = out[span_rows(span + reach), :].astype(F32)
        for far in range(1, reach + 1):
            own_rows = own_rows + picked(span, far) * out[span_rows(span + reach - far), :].astype(F32)
        mixed[span_rows(span), :] = own_rows.astype(BF16)
        return unused

    lax.fori_loop(reach, spans, mix, 0)

    @pl.when(place > 0)
    def _():
        for block in range(reach):
            before_copy(block).wait_recv()

    lax.fori_loop(0, reach, mix, 0)

    summed = grads[token_rows(me), :].astype(F32)
    for shift in range(1, groups):
        shares[shift - 1].wait_recv()
        summed = summed + parts[shift - 1].astype(F32)
    gb[...] = summed[:, :N]
    gc[...] = summed[:, N:]

    keep.wait()
    for copy in small + large + shares:
        copy.wait_send()
    for chunk in range(groups):

        @pl.when(me != chunk)
        def _(chunk=chunk):
            dx_copy(chunk).wait_send()
            remote(
                dx.at[pl.ds(0, tok_dev), :], gx.at[:, pl.ds(chunk * width, width)],
                z_send.at[4, chunk], z_recv.at[4, chunk], "head", chunk,
            ).wait_recv()

    @pl.when(place > 0)
    def _():
        for copy in later:
            copy.wait_send()

    @pl.when(place < ctx - 1)
    def _():
        for block in range(reach):
            before_copy(block).wait_send()

    for far in range(1, ctx):

        @pl.when(place >= far)
        def _(far=far):
            to_earlier[far - 1].wait_send()

        @pl.when(place + far < ctx)
        def _(far=far):
            to_later[far - 1].wait_send()


def body(channels, b_own, c_own, dt_own, a_log, skip_gain, mix_gain, offsets, cotangent):
    groups = lax.axis_size("head")
    ctx = lax.axis_size("ctx")
    tok_dev = channels.shape[0]
    tokens = tok_dev * groups
    spans = tokens // Q
    reach = spans // 2
    heads = a_log.shape[0]
    width = heads * P_SIZE
    in_scale = 1.0 / math.sqrt(N * tokens * ctx)
    pad = -(-heads // 16) * 16
    skip = jnp.repeat(skip_gain, P_SIZE)[None, :]
    gain = jnp.repeat(mix_gain.T, P_SIZE, axis=1)
    offs = jnp.pad(offsets, ((0, 0), (0, N - offsets.shape[1])))[:, None, :]
    held = pl.BlockSpec(memory_space=pl.ANY)
    here = pl.BlockSpec(memory_space=pltpu.VMEM)
    dma = pltpu.SemaphoreType.DMA
    args = (channels, b_own, c_own, dt_own, a_log[None, :], skip, gain, offs, cotangent)

    def kernel(*refs):
        mixer_kernel(groups, ctx, spans, reach, in_scale, *refs)

    return pl.pallas_call(
        kernel,
        out_shape=[
            jax.ShapeDtypeStruct((tokens, width), BF16),
            jax.ShapeDtypeStruct(channels.shape, BF16),
            jax.ShapeDtypeStruct((tok_dev, N), F32),
            jax.ShapeDtypeStruct((tok_dev, N), F32),
        ],
        in_specs=[held, held, held, held, here, here, here, held, held],
        out_specs=[here, held, here, here],
        scratch_shapes=[
            pltpu.VMEM(((spans + reach) * Q, width), BF16),
            pltpu.VMEM((spans + reach, 1, N), jnp.int32),
            pltpu.VMEM((tokens, N), BF16),
            pltpu.VMEM((tokens, N), BF16),
            pltpu.VMEM((tokens, dt_own.shape[1]), BF16),
            pltpu.VMEM((tokens, width), BF16),
            pltpu.VMEM((tokens, width), BF16),
            pltpu.VMEM((tokens, heads), F32),
            pltpu.VMEM((spans, heads, Q), F32),
            pltpu.VMEM((spans, width, N), BF16),
            pltpu.VMEM((width + pad, N), BF16),
            pltpu.VMEM((ctx - 1, width + pad, N), BF16),
            pltpu.VMEM((width + pad, N), BF16),
            pltpu.VMEM((ctx - 1, width + pad, N), BF16),
            pltpu.VMEM((spans, width, N), BF16),
            pltpu.VMEM((tokens, width), BF16),
            pltpu.VMEM((spans, width, N), F32),
            pltpu.VMEM((tokens, width), F32),
            pltpu.VMEM((tokens, N), F32),
            pltpu.VMEM((tokens, N), F32),
            pltpu.VMEM((tokens, 2 * N), BF16),
            pltpu.VMEM((groups - 1, tok_dev, 2 * N), BF16),
            pltpu.VMEM(((spans + reach) * Q, width), BF16),
            pltpu.VMEM((width, N), F32),
            pltpu.VMEM((heads, N), F32),
            dma((6, groups)),
            dma((6, groups)),
            dma((2, ctx)),
            dma((2, ctx)),
            dma((2 + reach,)),
            dma((2 + reach,)),
            dma((7,)),
        ],
        compiler_params=pltpu.CompilerParams(
            collective_id=0, has_side_effects=True, vmem_limit_bytes=VMEM_BYTES
        ),
    )(*args)


def solution(mesh):
    by_token = P(("ctx", "head"), None)
    return jax.shard_map(
        body,
        mesh=mesh,
        in_specs=(
            by_token, by_token, by_token, by_token, P("head"), P("head"), P("head", None),
            P("ctx", None), P("ctx", "head"),
        ),
        out_specs=(P("ctx", "head"), by_token, by_token, by_token),
        check_vma=False,
    )
```

```python
import math

import jax
import jax.numpy as jnp
from jax import lax
from jax.experimental import pallas as pl
from jax.experimental.pallas import tpu as pltpu
from jax.sharding import PartitionSpec as P

P_SIZE = 64
N = 128
Q = 128
F32 = jnp.float32
BF16 = jnp.bfloat16
VMEM_BYTES = 56 * 1024 * 1024


def dot(left, right, dims, precision=None):
    return lax.dot_general(
        left, right, (dims, ((), ())), preferred_element_type=F32, precision=precision
    )


def iota(shape, dim):
    return lax.broadcasted_iota(jnp.int32, shape, dim)


def halves(value):
    high = value.astype(BF16)
    return high, (value - high.astype(F32)).astype(BF16)


def head_of_column(heads):
    shape = (heads, heads * P_SIZE)
    first = iota(shape, 0) * P_SIZE
    column = iota(shape, 1)
    return ((column >= first) & (column < first + P_SIZE)).astype(F32).astype(BF16)


def over_columns(value, spread):
    high, low = halves(value)
    return dot(high, spread, ((1,), (0,))) + dot(low, spread, ((1,), (0,)))


def over_rows(column, spread):
    high, low = halves(jnp.broadcast_to(column, (column.shape[0], N)))
    return dot(spread, high, ((0,), (0,))) + dot(spread, low, ((0,), (0,)))


def two_heads(value):
    lower = iota(value.shape, 1) < P_SIZE
    zero = jnp.zeros_like(value)
    return jnp.concatenate([jnp.where(lower, value, zero), jnp.where(lower, zero, value)], axis=0)


def remote(source, target, send, recv, axis, place):
    return pltpu.make_async_remote_copy(
        src_ref=source,
        dst_ref=target,
        send_sem=send,
        recv_sem=recv,
        device_id={axis: place},
        device_id_type=pl.DeviceIdType.MESH,
    )


def mixer_kernel(
    groups, ctx, spans, reach, in_scale,
    chan_in, b_in, c_in, dt_in, a_log, skip, gain, offs, cot_in,
    mixed, gx, gb, gc,
    cot, off, b_all, c_all, dt_all, chan, g, cum_all, cumt_all, full, pay_g, other_g, both_g, ends_g, pay_s, other_s, both_s, ends_s,
    pieces, dx, starts, y_intra, db, dc, grads, parts, out, carry, running,
    z_send, z_recv, c_send, c_recv, n_send, n_recv, local,
):
    heads = a_log.shape[1]
    width = heads * P_SIZE
    tok_dev = chan_in.shape[0]
    slots = gain.shape[0]
    me = lax.axis_index("head")
    place = lax.axis_index("ctx")
    spread = head_of_column(heads)

    def token_rows(index):
        return pl.ds(pl.multiple_of(index * tok_dev, 64), tok_dev)

    def wide(index):
        return pl.ds(pl.multiple_of(index * width, 128), width)

    def span_rows(span):
        return pl.ds(pl.multiple_of(span * Q, Q), Q)

    barrier = pltpu.get_barrier_semaphore()
    for shift in range(1, groups):
        pl.semaphore_signal(
            barrier, inc=1, device_id={"head": lax.rem(me + shift, groups)},
            device_id_type=pl.DeviceIdType.MESH,
        )
    for shift in range(1, ctx):
        pl.semaphore_signal(
            barrier, inc=1, device_id={"ctx": lax.rem(place + shift, ctx)},
            device_id_type=pl.DeviceIdType.MESH,
        )
    own = [
        pltpu.make_async_copy(b_in, b_all.at[token_rows(me), :], local.at[0]),
        pltpu.make_async_copy(c_in, c_all.at[token_rows(me), :], local.at[1]),
        pltpu.make_async_copy(dt_in, dt_all.at[token_rows(me), :], local.at[2]),
        pltpu.make_async_copy(cot_in, cot.at[pl.ds(0, spans * Q), :], local.at[3]),
        pltpu.make_async_copy(offs, off.at[pl.ds(0, spans)], local.at[4]),
        pltpu.make_async_copy(chan_in.at[:, wide(me)], chan.at[token_rows(me), :], local.at[5]),
    ]
    for copy in own:
        copy.start()
    pl.semaphore_wait(barrier, groups - 1 + ctx - 1)

    small, large = [], []
    for shift in range(1, groups):
        target = lax.rem(me + shift, groups)
        for kind, (source, home) in enumerate(((b_in, b_all), (c_in, c_all), (dt_in, dt_all))):
            small.append(
                remote(
                    source, home.at[token_rows(me), :], z_send.at[kind, shift],
                    z_recv.at[kind, shift], "head", target,
                )
            )
        large.append(
            remote(
                chan_in.at[:, wide(target)], chan.at[token_rows(me), :], z_send.at[3, shift],
                z_recv.at[3, shift], "head", target,
            )
        )
    back = lax.rem(place + ctx - 1, ctx)
    onward = lax.rem(place + 1, ctx)
    later = [
        remote(
            offs.at[pl.ds(0, reach)], off.at[pl.ds(spans, reach)], n_send.at[0], n_recv.at[0],
            "ctx", back,
        ),
        remote(
            cot_in.at[pl.ds(0, reach * Q), :], cot.at[pl.ds(spans * Q, reach * Q), :],
            n_send.at[1], n_recv.at[1], "ctx", back,
        ),
    ]
    for copy in small:
        copy.start()

    @pl.when(place > 0)
    def _():
        for copy in later:
            copy.start()

    for copy in large:
        copy.start()

    @pl.when(place == 0)
    def _():
        out[pl.ds(0, reach * Q), :] = jnp.zeros((reach * Q, width), BF16)

    @pl.when(place == ctx - 1)
    def _():
        cot[pl.ds(spans * Q, reach * Q), :] = jnp.zeros((reach * Q, width), BF16)
        off[pl.ds(spans, reach)] = jnp.zeros((reach, 1, N), jnp.int32)

    for copy in own[:5]:
        copy.wait()
    for copy in small:
        copy.wait_recv()

    chosen = (
        iota((dt_all.shape[1], heads), 0) == iota((dt_all.shape[1], heads), 1) + me * heads
    ).astype(F32).astype(BF16)
    tri = (iota((Q, Q), 0) >= iota((Q, Q), 1)).astype(F32)
    rate = -jnp.exp(a_log[...])

    def add_up(span, total):
        rows = span_rows(span)
        steps = dot(dt_all[rows, :], chosen, ((1,), (0,)))
        decay = rate * (jnp.maximum(steps, 0.0) + jnp.log1p(jnp.exp(-jnp.abs(steps))))
        cumt = dot(decay, tri, ((0,), (1,)), lax.Precision.HIGHEST)
        cum_all[rows, :] = dot(tri, decay, ((1,), (0,)), lax.Precision.HIGHEST)
        cumt_all[span] = cumt
        return total + cumt[:, Q - 1 : Q]

    total = lax.fori_loop(0, spans, add_up, jnp.zeros((heads, 1), F32))
    pad = pay_g.shape[0] - width

    def log_rows(value):
        value = jnp.broadcast_to(value, (heads, N))
        high, low = halves(value)
        lowest = (value - high.astype(F32) - low.astype(F32)).astype(BF16)
        lane = iota((heads, N), 1)
        rows = jnp.where(lane == 0, high, jnp.where(lane == 1, low, lowest))
        if pad > heads:
            rows = jnp.concatenate([rows, jnp.zeros((pad - heads, N), BF16)], axis=0)
        return rows

    packed = log_rows(total)
    pay_g[pl.ds(width, pad), :] = packed
    core = lax.rem(place, 2)
    sibling = place + 1 - 2 * core
    pay_s[pl.ds(width, pad), :] = packed

    @pl.when(place < ctx - 1)
    def _():
        for copy in later:
            copy.wait_recv()

    def picked(row, far):
        offset = off[row]
        weight = jnp.zeros((1, width), F32)
        for slot in range(slots):
            hit = (offset[:, slot : slot + 1] == far).astype(F32)
            weight = weight + hit * gain[slot : slot + 1, :]
        return weight

    carry[...] = jnp.zeros_like(carry)

    def back_mix(span, earlier):
        rows = span_rows(span)
        grad = cot[rows, :].astype(F32)
        for far in range(1, reach + 1):
            grad = grad + picked(span + far, far) * cot[span_rows(span + far), :].astype(F32)
        grad = grad.astype(BF16)
        g[rows, :] = grad
        scaled = (grad.astype(F32) * over_columns(jnp.exp(cum_all[rows, :]), spread)).astype(BF16)
        flow = dot(scaled, c_all[rows, :], ((0,), (0,)))
        full[span] = flow.astype(BF16)
        carry[...] = carry[...] + over_rows(jnp.exp(earlier), spread) * flow
        return earlier + cumt_all[span][:, Q - 1 : Q]

    lax.fori_loop(0, spans, back_mix, jnp.zeros((heads, 1), F32))
    pay_g[pl.ds(0, width), :] = carry[...].astype(BF16)

    def scan_copies(kind, source, ends, sign):
        return [
            remote(
                source, ends.at[far - 1], c_send.at[kind, far], c_recv.at[kind, far], "ctx",
                lax.rem(place + ctx + 2 * sign * far, ctx),
            )
            for far in range(1, ctx // 2)
        ]

    to_earlier = scan_copies(0, both_g, ends_g, -1)
    to_later = scan_copies(1, both_s, ends_s, 1)

    def log_column(ref):
        logs = ref[pl.ds(width, pad), :].astype(F32)[:heads]
        return logs[:, 0:1] + logs[:, 1:2] + logs[:, 2:3]

    def pair_up(kind, pay, other, both, nearer):
        copy = remote(pay, other, c_send.at[kind, 0], c_recv.at[kind, 0], "ctx", sibling)
        copy.start()
        near = nearer.astype(F32)
        own_log = jnp.broadcast_to(total, (heads, N))[:, :1]
        copy.wait_recv()
        other_log = log_column(other)
        joint = over_rows(jnp.exp((1.0 - near) * other_log), spread) * pay[
            pl.ds(0, width), :
        ].astype(F32) + over_rows(jnp.exp(near * own_log), spread) * other[
            pl.ds(0, width), :
        ].astype(F32)
        both[pl.ds(0, width), :] = joint.astype(BF16)
        both[pl.ds(width, pad), :] = log_rows(own_log + other_log)
        return copy

    def gather_ends(other, nearer, ends, copies, present):
        near = nearer.astype(F32)
        carry[...] = near * other[pl.ds(0, width), :].astype(F32)
        running[...] = jnp.broadcast_to(near * log_column(other), running.shape)
        for far in range(1, ctx // 2):

            @pl.when(present(far))
            def _(far=far):
                copies[far - 1].wait_recv()
                sums = running[...]
                carry[...] = carry[...] + over_rows(jnp.exp(sums[:, :1]), spread) * ends[
                    far - 1, pl.ds(0, width), :
                ].astype(F32)
                logs = ends[far - 1, pl.ds(width, pad), :].astype(F32)[:heads]
                running[...] = sums + (logs[:, 0:1] + logs[:, 1:2] + logs[:, 2:3])

    pair_g = pair_up(0, pay_g, other_g, both_g, core == 0)
    for far in range(1, ctx // 2):

        @pl.when(place >= 2 * far)
        def _(far=far):
            to_earlier[far - 1].start()

    own[5].wait()
    for copy in large:
        copy.wait_recv()

    def tail_of(rows):
        cum = cum_all[rows, :]
        last = cum[Q - 1 : Q, :]
        return over_columns(jnp.exp(last - cum) * in_scale, spread)

    carry[...] = jnp.zeros_like(carry)

    def add_pieces(span, unused):
        rows = span_rows(span)
        state = carry[...]
        starts[span] = state
        scaled = (chan[rows, :].astype(F32) * tail_of(rows)).astype(BF16)
        added = dot(scaled, b_all[rows, :], ((0,), (0,)))
        carry[...] = over_rows(jnp.exp(cumt_all[span][:, Q - 1 : Q]), spread) * state + added
        return unused

    lax.fori_loop(0, spans, add_pieces, 0)
    pay_s[pl.ds(0, width), :] = carry[...].astype(BF16)
    pair_s = pair_up(1, pay_s, other_s, both_s, core == 1)
    for far in range(1, ctx // 2):

        @pl.when(place // 2 + far < ctx // 2)
        def _(far=far):
            to_later[far - 1].start()

    gather_ends(other_g, core == 0, ends_g, to_earlier, lambda far: place // 2 + far < ctx // 2)

    def dx_copy(chunk):
        return remote(
            dx.at[pl.ds(chunk * tok_dev, tok_dev), :], gx.at[:, wide(me)], z_send.at[4, chunk],
            z_recv.at[4, me], "head", chunk,
        )

    def grad_channels(step, unused):
        span = spans - 1 - step
        rows = span_rows(span)
        after = carry[...]
        flow = after.astype(BF16)
        pieces[span] = flow
        b_rows = b_all[rows, :]
        cum = cum_all[rows, :]
        cumt = cumt_all[span]
        from_state = dot(b_rows, flow, ((1,), (1,))) * tail_of(rows)
        scores = dot(b_rows, c_all[rows, :], ((1,), (1,))) * in_scale
        seen = iota((Q, Q), 0) <= iota((Q, Q), 1)
        for pair in range(heads // 2):
            columns = slice(pair * 2 * P_SIZE, (pair + 1) * 2 * P_SIZE)
            weights = []
            for head in (2 * pair, 2 * pair + 1):
                gap = cumt[head : head + 1, :] - cum[:, head : head + 1]
                weights.append((scores * jnp.exp(jnp.where(seen, gap, -1e30))).astype(BF16))
            part = g[rows, columns]
            intra = dot(jnp.concatenate(weights, axis=1), two_heads(part), ((1,), (0,)))
            dx[rows, columns] = (
                intra + from_state[:, columns] + skip[:, columns] * part.astype(F32)
            ).astype(BF16)
        carry[...] = full[span].astype(F32) + over_rows(jnp.exp(cumt[:, Q - 1 : Q]), spread) * after
        for chunk in range(groups):

            @pl.when((span == chunk * tok_dev // Q) & (me != chunk))
            def _(chunk=chunk):
                dx_copy(chunk).start()

        return unused

    lax.fori_loop(0, spans, grad_channels, 0)
    keep = pltpu.make_async_copy(dx.at[token_rows(me), :], gx.at[:, wide(me)], local.at[6])
    keep.start()

    def intra(span, unused):
        rows = span_rows(span)
        b_rows = b_all[rows, :]
        c_rows = c_all[rows, :]
        cum = cum_all[rows, :]
        cumt = cumt_all[span]
        scores = dot(c_rows, b_rows, ((1,), (1,))) * in_scale
        seen = iota((Q, Q), 0) >= iota((Q, Q), 1)
        score_grads = jnp.zeros((Q, Q), F32)
        for pair in range(heads // 2):
            columns = slice(pair * 2 * P_SIZE, (pair + 1) * 2 * P_SIZE)
            chans = chan[rows, columns]
            products = dot(two_heads(g[rows, columns]), chans, ((1,), (1,)))
            weights = []
            for one, head in enumerate((2 * pair, 2 * pair + 1)):
                gap = cum[:, head : head + 1] - cumt[head : head + 1, :]
                decay = jnp.exp(jnp.where(seen, gap, -1e30))
                weights.append((scores * decay).astype(BF16))
                score_grads = score_grads + products[one * Q : (one + 1) * Q, :] * decay
            y_intra[rows, columns] = dot(
                jnp.concatenate(weights, axis=1), two_heads(chans), ((1,), (0,))
            ) + skip[:, columns] * chans.astype(F32)
        score_grads = (score_grads * in_scale).astype(BF16)
        scaled = (chan[rows, :].astype(F32) * tail_of(rows)).astype(BF16)
        dc[rows, :] = dot(score_grads, b_rows, ((1,), (0,)))
        db[rows, :] = dot(score_grads, c_rows, ((0,), (0,))) + dot(
            scaled, pieces[span], ((1,), (0,))
        )
        return unused

    lax.fori_loop(0, spans, intra, 0)

    gather_ends(other_s, core == 1, ends_s, to_later, lambda far: place >= 2 * far)

    def before_copy(block):
        return remote(
            out.at[pl.ds((spans + block) * Q, Q), :], out.at[pl.ds(block * Q, Q), :],
            n_send.at[2 + block], n_recv.at[2 + block], "ctx", onward,
        )

    def outputs(span, unused):
        rows = span_rows(span)
        state = carry[...]
        whole = (starts[span] + state).astype(BF16)
        grown = over_columns(jnp.exp(cum_all[rows, :]), spread)
        out[span_rows(span + reach), :] = (
            y_intra[rows, :] + dot(c_all[rows, :], whole, ((1,), (1,))) * grown
        ).astype(BF16)
        for block in range(reach):

            @pl.when((span == spans - reach + block) & (place < ctx - 1))
            def _(block=block):
                before_copy(block).start()

        scaled = (g[rows, :].astype(F32) * grown).astype(BF16)
        grads[rows, pl.ds(0, N)] = db[rows, :].astype(BF16)
        grads[rows, pl.ds(N, N)] = (dc[rows, :] + dot(scaled, whole, ((1,), (0,)))).astype(BF16)
        carry[...] = over_rows(jnp.exp(cumt_all[span][:, Q - 1 : Q]), spread) * state
        return unused

    lax.fori_loop(0, spans, outputs, 0)
    shares = [
        remote(
            grads.at[token_rows(lax.rem(me + shift, groups)), :], parts.at[shift - 1],
            z_send.at[5, shift], z_recv.at[5, shift], "head", lax.rem(me + shift, groups),
        )
        for shift in range(1, groups)
    ]
    for copy in shares:
        copy.start()

    def mix(span, unused):
        own_rows = out[span_rows(span + reach), :].astype(F32)
        for far in range(1, reach + 1):
            own_rows = own_rows + picked(span, far) * out[span_rows(span + reach - far), :].astype(F32)
        mixed[span_rows(span), :] = own_rows.astype(BF16)
        return unused

    lax.fori_loop(reach, spans, mix, 0)

    @pl.when(place > 0)
    def _():
        for block in range(reach):
            before_copy(block).wait_recv()

    lax.fori_loop(0, reach, mix, 0)

    summed = grads[token_rows(me), :].astype(F32)
    for shift in range(1, groups):
        shares[shift - 1].wait_recv()
        summed = summed + parts[shift - 1].astype(F32)
    gb[...] = summed[:, :N]
    gc[...] = summed[:, N:]

    keep.wait()
    pair_g.wait_send()
    pair_s.wait_send()
    for copy in small + large + shares:
        copy.wait_send()
    for chunk in range(groups):

        @pl.when(me != chunk)
        def _(chunk=chunk):
            dx_copy(chunk).wait_send()
            remote(
                dx.at[pl.ds(0, tok_dev), :], gx.at[:, pl.ds(chunk * width, width)],
                z_send.at[4, chunk], z_recv.at[4, chunk], "head", chunk,
            ).wait_recv()

    @pl.when(place > 0)
    def _():
        for copy in later:
            copy.wait_send()

    @pl.when(place < ctx - 1)
    def _():
        for block in range(reach):
            before_copy(block).wait_send()

    for far in range(1, ctx // 2):

        @pl.when(place >= 2 * far)
        def _(far=far):
            to_earlier[far - 1].wait_send()

        @pl.when(place // 2 + far < ctx // 2)
        def _(far=far):
            to_later[far - 1].wait_send()


def body(channels, b_own, c_own, dt_own, a_log, skip_gain, mix_gain, offsets, cotangent):
    groups = lax.axis_size("head")
    ctx = lax.axis_size("ctx")
    tok_dev = channels.shape[0]
    tokens = tok_dev * groups
    spans = tokens // Q
    reach = spans // 2
    heads = a_log.shape[0]
    width = heads * P_SIZE
    in_scale = 1.0 / math.sqrt(N * tokens * ctx)
    pad = -(-heads // 16) * 16
    skip = jnp.repeat(skip_gain, P_SIZE)[None, :]
    gain = jnp.repeat(mix_gain.T, P_SIZE, axis=1)
    offs = jnp.pad(offsets, ((0, 0), (0, N - offsets.shape[1])))[:, None, :]
    held = pl.BlockSpec(memory_space=pl.ANY)
    here = pl.BlockSpec(memory_space=pltpu.VMEM)
    dma = pltpu.SemaphoreType.DMA
    args = (channels, b_own, c_own, dt_own, a_log[None, :], skip, gain, offs, cotangent)

    def kernel(*refs):
        mixer_kernel(groups, ctx, spans, reach, in_scale, *refs)

    return pl.pallas_call(
        kernel,
        out_shape=[
            jax.ShapeDtypeStruct((tokens, width), BF16),
            jax.ShapeDtypeStruct(channels.shape, BF16),
            jax.ShapeDtypeStruct((tok_dev, N), F32),
            jax.ShapeDtypeStruct((tok_dev, N), F32),
        ],
        in_specs=[held, held, held, held, here, here, here, held, held],
        out_specs=[here, held, here, here],
        scratch_shapes=[
            pltpu.VMEM(((spans + reach) * Q, width), BF16),
            pltpu.VMEM((spans + reach, 1, N), jnp.int32),
            pltpu.VMEM((tokens, N), BF16),
            pltpu.VMEM((tokens, N), BF16),
            pltpu.VMEM((tokens, dt_own.shape[1]), BF16),
            pltpu.VMEM((tokens, width), BF16),
            pltpu.VMEM((tokens, width), BF16),
            pltpu.VMEM((tokens, heads), F32),
            pltpu.VMEM((spans, heads, Q), F32),
            pltpu.VMEM((spans, width, N), BF16),
            pltpu.VMEM((width + pad, N), BF16),
            pltpu.VMEM((width + pad, N), BF16),
            pltpu.VMEM((width + pad, N), BF16),
            pltpu.VMEM((ctx // 2 - 1, width + pad, N), BF16),
            pltpu.VMEM((width + pad, N), BF16),
            pltpu.VMEM((width + pad, N), BF16),
            pltpu.VMEM((width + pad, N), BF16),
            pltpu.VMEM((ctx // 2 - 1, width + pad, N), BF16),
            pltpu.VMEM((spans, width, N), BF16),
            pltpu.VMEM((tokens, width), BF16),
            pltpu.VMEM((spans, width, N), F32),
            pltpu.VMEM((tokens, width), F32),
            pltpu.VMEM((tokens, N), F32),
            pltpu.VMEM((tokens, N), F32),
            pltpu.VMEM((tokens, 2 * N), BF16),
            pltpu.VMEM((groups - 1, tok_dev, 2 * N), BF16),
            pltpu.VMEM(((spans + reach) * Q, width), BF16),
            pltpu.VMEM((width, N), F32),
            pltpu.VMEM((heads, N), F32),
            dma((6, groups)),
            dma((6, groups)),
            dma((2, ctx)),
            dma((2, ctx)),
            dma((2 + reach,)),
            dma((2 + reach,)),
            dma((7,)),
        ],
        compiler_params=pltpu.CompilerParams(
            collective_id=0, has_side_effects=True, vmem_limit_bytes=VMEM_BYTES
        ),
    )(*args)


def solution(mesh):
    by_token = P(("ctx", "head"), None)
    return jax.shard_map(
        body,
        mesh=mesh,
        in_specs=(
            by_token, by_token, by_token, by_token, P("head"), P("head"), P("head", None),
            P("ctx", None), P("ctx", "head"),
        ),
        out_specs=(P("ctx", "head"), by_token, by_token, by_token),
        check_vma=False,
    )
```
